32 devices in a mesh: groups: 2 (over y), tm: 4 (over z), archive: 2 (over x), replica: 2 (over core).
Axes of the slice: x: 2, y: 2, z: 4, core: 2. Of those that a mesh axis runs over, the one named last changes fastest.
Arguments:
- seeds: float32 [4, 2048, 256], P(('groups', 'archive'), 'tm', 'replica'), parts along dimension 0, may hold values from 0.01 to 1
- band: bfloat16 [4, 16, 3, 128, 128], P(('groups', 'archive'), 'tm'), parts along dimension 0, may hold values from 9.9658966e-05 to 1
- band_mask: int32 [4, 16, 3], P(('groups', 'archive'), 'tm'), parts along dimension 0, may hold values 0 or 1
- recording: int32 [4, 2048], P(('groups', 'archive'), 'tm'), parts along dimension 0, may hold values from 0 to 15, never falling along the last dimension, each value on 1 to 256 neighbouring positions
- cross: bfloat16 [4, 16, 28, 128, 128], P(('groups', 'archive'), 'tm'), parts along dimension 0, may hold values from 9.9658966e-05 to 1
- cross_ref: int32 [4, 16, 28], P(('groups', 'archive'), 'tm'), parts along dimension 0, may hold values from 0 to 31, as said below
- cross_mask: int32 [4, 16, 28], P(('groups', 'archive'), 'tm'), parts along dimension 0, may hold values 0 or 1
Outputs:
- labels: float32 [4, 2048, 256], P(('groups', 'archive'), 'tm', 'replica'), parts along dimension 0
- change: float32 [4], P('groups'), parts along dimension 0
The draws below stay inside these ranges and needn't reach their ends.
There are 2 independent parts, one for each index of `groups`. The reference program is written for one: setup_inputs(seed, part) draws one part's arguments, and reference() takes and returns one part's arrays. A program takes and returns all parts, laid end to end along the dimension named above; each array names one. Nothing has to cross between parts.
Inputs may be any that keep to these rules, and one draw needn't show every extreme that they name: `cross_ref`: the 112 listed blocks of the rows of one index pair of tm and archive lie in the rows of other index pairs, and at most 16 of them lie in the 512 rows of any one such index pair, a bound reached on every device.
All inputs are finite; a program needn't handle non-finite values. No bound on the sum of `band_mask` or of `cross_mask` on one device may be relied on, other than what follows from the above.
Results may differ from the reference program's by a relative error of at most 0.0003.
Values may be sent and summed in bfloat16 or wider, within the bound.
A program may use at most 64 MiB of HBM per device.

```python
import math
import jax
import jax.numpy as jnp
import numpy as np
from jax import lax

L = 256
BLOCK = 128
ROWS_DEV = 512
CROSS = 28
ITERS = 2
SEG = 2048
NBA = 16
N_TM = 4
N_ARCHIVE = 2


def draw_cross_ref(key, part):
    key = jax.random.fold_in(key, 11)
    nblk = ROWS_DEV // BLOCK
    slots = nblk * CROSS
    total = N_ARCHIVE * N_TM
    peers = total - 1
    half = total // 2

    def one_device(device):
        sub = jax.random.fold_in(key, device)
        first, second, third = jax.random.split(sub, 3)
        own_arch = device // N_TM
        own_tm = device % N_TM
        joined = own_tm * N_ARCHIVE + own_arch
        offsets = jax.random.permutation(first, peers) + 1
        head = offsets[0]
        offsets = jnp.where(offsets == half, head, offsets)
        offsets = offsets.at[0].set(half)
        spots = jax.random.permutation(second, slots)
        offset = offsets[spots % peers]
        target = (joined + offset) % total
        owner_tm = target // N_ARCHIVE
        other = target % N_ARCHIVE
        within = jax.random.randint(third, (slots,), 0, nblk)
        return other * (nblk * N_TM) + owner_tm * nblk + within
    table = jax.vmap(one_device)(jnp.arange(N_ARCHIVE * N_TM))
    return table.reshape(N_ARCHIVE, N_TM * nblk, CROSS).astype(jnp.int32)


def set_ends(array, stream_key, least, largest):
    spot = [jax.random.randint(jax.random.fold_in(stream_key, axis), (), 0, length) for axis, length in enumerate(array.shape)]
    widest = array.shape.index(max(array.shape))
    beside = spot[:widest] + [(spot[widest] + 1) % array.shape[widest]] + spot[widest + 1:]
    return array.at[tuple(spot)].set(least).at[tuple(beside)].set(largest)


def levels(rng, dims, cuts, least, top_value):
    gain, own = 1.0, jax.random.fold_in(rng, 6)
    for position, parts in cuts:
        draws = jnp.exp(jax.random.uniform(jax.random.fold_in(own, position), (parts,), jnp.float32, least / len(cuts), top_value / len(cuts)))
        gain = gain * jnp.repeat(draws, dims[position] // parts).reshape([-1 if axis == position else 1 for axis in range(len(dims))])
    return gain


def length_profile(count, total, most, lean):
    weights = [(1 << 20) // math.isqrt(rank ** lean) + 1 for rank in range(2, count + 1)]
    spare, holding = total - most - (count - 1), [1] * (count - 1)
    while spare > 0:
        free = [i for i in range(count - 1) if holding[i] < most]
        mass, left = sum([weights[i] for i in free]), spare
        for i in free:
            addition = min(most - holding[i], max(1, left * weights[i] // mass), spare)
            holding[i] = holding[i] + addition
            spare = spare - addition
    return np.array([most] + holding)


def uneven(own_key, number_of, total, bound, slope):
    if number_of == 2:
        one = jax.random.randint(own_key, (), max(1, total - bound), min(bound, total - 1) + 1)
        return jnp.stack([one, total - one])
    sizes = jnp.asarray(length_profile(number_of, total, bound, slope), jnp.int32)
    pairs = (number_of - 1) // 2
    source_of, taker = sizes[1:1 + 2 * pairs:2], sizes[2:2 + 2 * pairs:2]
    slack = jnp.minimum(source_of - 1, bound - taker)
    passed = jax.random.randint(jax.random.fold_in(own_key, 1), (pairs,), 0, 1 << 20) % (slack + 1)
    sizes = sizes.at[1:1 + 2 * pairs:2].set(source_of - passed).at[2:2 + 2 * pairs:2].set(taker + passed)
    return sizes[jax.random.permutation(jax.random.fold_in(own_key, 2), number_of)]


def setup_inputs(seed: int = 0, part: int = 0) -> dict:
    streams_of = jax.random.split(jax.random.key(seed), 8)
    part_splits = jax.random.split(jax.random.fold_in(streams_of[7], part), 8)
    seeds = jnp.clip(jnp.exp(math.log(1.0) - 4.6051702 * jax.random.uniform(part_splits[0], (N_ARCHIVE, SEG, L), jnp.float32) ** levels(part_splits[0], (N_ARCHIVE, SEG, L), ((0, 2), (1, 4), (2, 2)), -0.2, 0.2)), 0.01, 1.0)
    band = jnp.clip(jnp.exp(math.log(1.0) - 9.213757 * jax.random.uniform(part_splits[1], (N_ARCHIVE, NBA, 3, BLOCK, BLOCK), jnp.float32) ** levels(part_splits[1], (N_ARCHIVE, NBA, 3, BLOCK, BLOCK), ((0, 2), (1, 4)), -0.2, 0.2)), 9.965896606445312e-05, 1.0).astype(jnp.bfloat16)
    band_mask = set_ends((jax.random.randint(part_splits[2], (N_ARCHIVE, NBA, 3), 0, 4) < 3).astype(jnp.int32), jax.random.fold_in(part_splits[2], 1), 0, 1)
    recording = jax.vmap(lambda own: jnp.searchsorted(jnp.cumsum(uneven(own, 4 * N_TM, SEG, ROWS_DEV // 2, 2)), jnp.arange(SEG), side="right"))(jax.random.split(part_splits[3], N_ARCHIVE)).reshape((N_ARCHIVE, SEG)).astype(jnp.int32)
    cross = jnp.clip(jnp.exp(math.log(1.0) - 9.213757 * jax.random.uniform(part_splits[4], (N_ARCHIVE, NBA, CROSS, BLOCK, BLOCK), jnp.float32) ** levels(part_splits[4], (N_ARCHIVE, NBA, CROSS, BLOCK, BLOCK), ((0, 2), (1, 4)), -0.2, 0.2)), 9.965896606445312e-05, 1.0).astype(jnp.bfloat16)
    cross_ref = draw_cross_ref(jax.random.fold_in(jax.random.fold_in(streams_of[7], part), 71), part)
    cross_mask = set_ends((jax.random.randint(part_splits[6], (N_ARCHIVE, NBA, CROSS), 0, 2) < 1).astype(jnp.int32), jax.random.fold_in(part_splits[6], 1), 0, 1)
    return {"seeds": seeds, "band": band, "band_mask": band_mask, "recording": recording, "cross": cross, "cross_ref": cross_ref, "cross_mask": cross_mask}


ALPHA = 0.85


def reference(seeds, band, band_mask, recording, cross, cross_ref, cross_mask):
    narch, seg, width = seeds.shape
    nba = seg // BLOCK
    recb = recording.reshape(narch, nba, BLOCK)
    edge = jnp.full((narch, 1, BLOCK), -1, jnp.int32)
    recp = jnp.concatenate([edge, recb, edge], axis=1)
    cols = jnp.stack([recp[:, 0:nba], recp[:, 1:nba + 1], recp[:, 2:nba + 2]], axis=2)
    keep = (recb[:, :, None, :, None] == cols[:, :, :, None, :]) & (band_mask[:, :, :, None, None] > 0)
    band_w = jnp.where(keep, band, jnp.zeros((), jnp.bfloat16))
    live = cross_mask > 0
    cross_w = jnp.where(live[..., None, None], cross, jnp.zeros((), jnp.bfloat16))
    degree = jnp.sum(band_w.astype(jnp.float32), axis=(2, 4)) + jnp.sum(cross_w.astype(jnp.float32), axis=(2, 4))
    degree = degree.reshape(narch, seg, 1)
    current = seeds
    changes = []
    for step in range(ITERS):
        rounded = current.astype(jnp.bfloat16).reshape(narch, nba, BLOCK, width)
        flat = rounded.reshape(narch * nba, BLOCK, width)
        zero_block = jnp.zeros((narch, 1, BLOCK, width), jnp.bfloat16)
        padded = jnp.concatenate([zero_block, rounded, zero_block], axis=1)
        near = jnp.stack([padded[:, 0:nba], padded[:, 1:nba + 1], padded[:, 2:nba + 2]], axis=2)

        def per_archive(items):
            bweight, nearby, cweight, refs = items
            near_sum = jnp.einsum('boij,bojc->bic', bweight.astype(jnp.float32), nearby.astype(jnp.float32))
            panels = flat[refs]
            far_sum = jnp.einsum('bkij,bkjc->bic', cweight.astype(jnp.float32), panels.astype(jnp.float32))
            return near_sum + far_sum

        spread = lax.map(per_archive, (band_w, near, cross_w, cross_ref)).reshape(narch, seg, width)
        updated = (1.0 - ALPHA) * seeds + ALPHA * (current + spread) / (1.0 + degree)
        changes.append(jnp.sum(jnp.square(updated - current)) / (narch * seg * width))
        current = updated
    return current, jnp.stack(changes).astype(jnp.float32)
```

```python
import functools

import jax
import jax.numpy as jnp
from jax import lax
from jax.experimental import pallas as pl
from jax.experimental.pallas import tpu as pltpu
from jax.sharding import PartitionSpec as P

ITERS = 2
ALPHA = 0.85


def each(lo, hi, body):
    if hi - lo <= 4:
        for i in range(lo, hi):
            body(i)
    else:
        lax.fori_loop(lo, hi, lambda i, c: (body(i), c)[1], 0)


def kernel(
    dims,
    seeds,
    band,
    band_mask,
    recording,
    cross,
    cross_ref,
    cross_mask,
    out,
    change,
    lab0,
    lab1,
    cross_v,
    band_v,
    rec_s,
    rec_halo,
    current,
    scale,
    chg,
    in_sem,
    zs,
    zr,
    xs,
    xr,
    rs,
    rr,
    cs,
    cr,
    out_sem,
):
    n_tm, n_arch, n_rep, nblk, block, slots, nsub, group = dims
    labs = (lab0, lab1)
    per = nblk // nsub
    t = lax.axis_index("tm")
    a = lax.axis_index("archive")
    r = lax.axis_index("replica")
    total = n_tm * n_arch * n_rep
    me = (t * n_arch + a) * n_rep + r
    zero_slot = n_arch * n_tm * nblk
    own = (a * n_tm + t) * nblk
    archive_lo = a * n_tm * nblk
    archive_hi = archive_lo + n_tm * nblk - 1
    MESH = pl.DeviceIdType.MESH

    def peer(step):
        other = lax.rem(me + step, total)
        return {
            "tm": other // (n_arch * n_rep),
            "archive": lax.rem(other // n_rep, n_arch),
            "replica": lax.rem(other, n_rep),
        }

    loads = [pltpu.make_async_copy(band.at[0], band_v, in_sem.at[0])]
    for b in range(nblk):
        loads.append(pltpu.make_async_copy(cross.at[0, b], cross_v.at[b], in_sem.at[1 + b]))

    rec_halo[...] = jnp.full(rec_halo.shape, -1, jnp.int32)

    barrier = pltpu.get_barrier_semaphore()

    def greet(step):
        pl.semaphore_signal(barrier, inc=1, device_id=peer(step), device_id_type=MESH)

    each(1, total, greet)
    for b in range(nblk):
        rec_s[b] = jnp.broadcast_to(recording[:, b * block : (b + 1) * block], (8, block))
        lab0[own + b] = seeds[0, b * block : (b + 1) * block, :].astype(jnp.bfloat16)
    zeros = jnp.zeros((block, lab0.shape[2]), jnp.bfloat16)
    lab0[zero_slot] = zeros
    lab1[zero_slot] = zeros
    for load in loads:
        load.start()
    pl.semaphore_wait(barrier, total - 1)

    def z_copy(it, d, j, sub):
        src = t - j if d == 0 else t + j
        nxt = lax.rem(t + 1, n_tm) if d == 0 else lax.rem(t + n_tm - 1, n_tm)
        lab = labs[it]
        where = pl.ds((a * n_tm + src) * nblk + sub * per, per)
        return pltpu.make_async_remote_copy(
            src_ref=lab.at[where],
            dst_ref=lab.at[where],
            send_sem=zs.at[it, d, j, sub],
            recv_sem=zr.at[it, d, j + 1, sub],
            device_id={"tm": nxt},
            device_id_type=MESH,
        )

    def z_arrive(it, d, j, sub):
        src = t - j if d == 0 else t + j
        lab = labs[it]
        where = pl.ds((a * n_tm + src) * nblk + sub * per, per)
        return pltpu.make_async_remote_copy(
            src_ref=lab.at[where],
            dst_ref=lab.at[where],
            send_sem=zs.at[it, d, j, sub],
            recv_sem=zr.at[it, d, j, sub],
            device_id={"tm": lax.rem(t + 1, n_tm)},
            device_id_type=MESH,
        )

    def x_copy(it, m, src, sub):
        lab = labs[it]
        where = pl.ds((a * n_tm + src) * nblk + sub * per, per)
        return pltpu.make_async_remote_copy(
            src_ref=lab.at[where],
            dst_ref=lab.at[where],
            send_sem=xs.at[it, m, src, sub],
            recv_sem=xr.at[it, m, src, sub],
            device_id={"archive": lax.rem(a + m, n_arch)},
            device_id_type=MESH,
        )

    def x_arrive(it, m, src, sub):
        lab = labs[it]
        frm = lax.rem(a + n_arch - m, n_arch)
        where = pl.ds((frm * n_tm + src) * nblk + sub * per, per)
        return pltpu.make_async_remote_copy(
            src_ref=lab.at[where],
            dst_ref=lab.at[where],
            send_sem=xs.at[it, m, src, sub],
            recv_sem=xr.at[it, m, src, sub],
            device_id={"archive": lax.rem(a + m, n_arch)},
            device_id_type=MESH,
        )

    def has_next(d):
        return t + 1 < n_tm if d == 0 else t >= 1

    def has_source(d, j):
        return t >= j if d == 0 else t + j < n_tm

    def own_send(it, sub):
        for d in range(2):
            pl.when(has_next(d))(lambda d=d: z_copy(it, d, 0, sub).start())
        each(1, n_arch, lambda m: x_copy(it, m, t, sub).start())

    def hand_on(it, j, sub):
        for d in range(2):

            @pl.when(has_source(d, j))
            def _():
                src = t - j if d == 0 else t + j
                z_arrive(it, d, j, sub).wait_recv()
                pl.when(has_next(d))(lambda: z_copy(it, d, j, sub).start())
                each(1, n_arch, lambda m: x_copy(it, m, src, sub).start())

    def x_wait(it):
        def one(src):
            for sub in range(nsub):
                each(1, n_arch, lambda m: x_arrive(it, m, src, sub).wait_recv())

        each(0, n_tm, one)

    def drain(it):
        def one(src):
            for sub in range(nsub):
                each(1, n_arch, lambda m: x_copy(it, m, src, sub).wait_send())

        each(0, n_tm, one)

        def hop(j):
            for d in range(2):
                go = has_next(d) & has_source(d, j)

                @pl.when(go)
                def _():
                    for sub in range(nsub):
                        z_copy(it, d, j, sub).wait_send()

        each(0, n_tm, hop)

    def rec_copy(d):
        return pltpu.make_async_remote_copy(
            src_ref=rec_s.at[nblk - 1 if d == 0 else 0],
            dst_ref=rec_halo.at[d],
            send_sem=rs.at[d],
            recv_sem=rr.at[d],
            device_id={"tm": lax.rem(t + 1, n_tm) if d == 0 else lax.rem(t + n_tm - 1, n_tm)},
            device_id_type=MESH,
        )

    for d in range(2):
        pl.when(has_next(d))(lambda d=d: rec_copy(d).start())
    for sub in range(nsub):
        own_send(0, sub)

    def rows(b):
        return pl.ds(b * block, block)


    def cross_degree(b):
        loads[1 + b].wait()
        acc = jnp.zeros((block, block), jnp.float32)
        for k in range(slots):
            live = (cross_mask[0, b, k] > 0).astype(jnp.float32)
            acc += cross_v[b, k].astype(jnp.float32) * live
        scale[rows(b), :] = acc

    def band_weights(b):
        acc = scale[rows(b), :]
        mine = jnp.broadcast_to(rec_s[b, 0:1, :], (block, block)).astype(jnp.float32).T
        for o in range(3):
            near = b + o - 1
            if near < 0:
                theirs = rec_halo[0, 0:1, :]
            elif near >= nblk:
                theirs = rec_halo[1, 0:1, :]
            else:
                theirs = rec_s[near, 0:1, :]
            theirs = jnp.where(band_mask[0, b, o] > 0, theirs, -2).astype(jnp.float32)
            w = jnp.where(mine == theirs, band_v[b, o].astype(jnp.float32), 0.0)
            band_v[b, o] = w.astype(jnp.bfloat16)
            acc += w
        degree = jnp.sum(acc, axis=1, keepdims=True)
        scale[rows(b), :] = jnp.broadcast_to(ALPHA / (1.0 + degree), (block, scale.shape[1]))

    def spread_of(it, b):
        lab = labs[it]
        near = [jnp.clip(own + b + o - 1, archive_lo, archive_hi) for o in range(3)]
        acc = jnp.dot(
            jnp.concatenate([band_v[b, o] for o in range(3)], axis=1),
            jnp.concatenate([lab[i] for i in near], axis=0),
            preferred_element_type=jnp.float32,
        )
        for k0 in range(0, slots, group):
            ks = range(k0, k0 + group)
            spots = [jnp.where(cross_mask[0, b, k] > 0, cross_ref[0, b, k], zero_slot) for k in ks]
            acc += jnp.dot(
                jnp.concatenate([cross_v[b, k] for k in ks], axis=1),
                jnp.concatenate([lab[i] for i in spots], axis=0),
                preferred_element_type=jnp.float32,
            )
        return acc

    def step(it, b):
        spread = spread_of(it, b)
        first = seeds[0, rows(b), :]
        before = first if it == 0 else current[rows(b), :]
        updated = (1.0 - ALPHA) * first + (before + spread) * scale[rows(b), :]
        current[rows(b), :] = updated
        if it + 1 < ITERS:
            labs[it + 1][own + b] = updated.astype(jnp.bfloat16)
        diff = updated - before
        return jnp.sum(diff * diff, axis=0, keepdims=True)

    work = [functools.partial(cross_degree, b) for b in range(nblk)]
    for j_sub in range(nsub):
        if work:
            work.pop(0)()
        hand_on(0, 1, j_sub)
    for f in work:
        f()
    for d in range(2):
        came = has_source(d, 1)
        pl.when(came)(lambda d=d: rec_copy(d).wait_recv())
    loads[0].wait()
    work = [functools.partial(band_weights, b) for b in range(nblk)]

    def later(it, lo):
        def one(j):
            for sub in range(nsub):
                hand_on(it, j, sub)

        each(lo, n_tm, one)

    if n_tm > 2 and n_tm <= 6:
        for sub in range(nsub):
            hand_on(0, 2, sub)
            if work:
                work.pop(0)()
        for f in work:
            f()
        later(0, 3)
    else:
        for f in work:
            f()
        later(0, 2)
    x_wait(0)

    sums = jnp.zeros((1, seeds.shape[2]), jnp.float32)
    for sub in range(nsub):
        for b in range(sub * per, (sub + 1) * per):
            sums += step(0, b)
        own_send(1, sub)
        if sub >= 1:
            hand_on(1, 1, sub - 1)
    hand_on(1, 1, nsub - 1)
    later(1, 2)
    x_wait(1)
    totals = [sums]
    sums = jnp.zeros((1, seeds.shape[2]), jnp.float32)
    writes = []
    for b in range(nblk):
        sums += step(1, b)
        writes.append(
            pltpu.make_async_copy(current.at[rows(b)], out.at[0, rows(b)], out_sem.at[b])
        )
        writes[-1].start()
    totals.append(sums)

    row = lax.broadcasted_iota(jnp.int32, (8, seeds.shape[2]), 0)
    chg[me] = jnp.where(row == 0, totals[0], jnp.where(row == 1, totals[1], 0.0))

    def chg_copy(s):
        return pltpu.make_async_remote_copy(
            src_ref=chg.at[me],
            dst_ref=chg.at[me],
            send_sem=cs.at[s],
            recv_sem=cr.at[s],
            device_id=peer(s),
            device_id_type=MESH,
        )

    def chg_arrive(s):
        frm = lax.rem(me + total - s, total)
        return pltpu.make_async_remote_copy(
            src_ref=chg.at[frm],
            dst_ref=chg.at[frm],
            send_sem=cs.at[s],
            recv_sem=cr.at[s],
            device_id=peer(s),
            device_id_type=MESH,
        )

    each(1, total, lambda s: chg_copy(s).start())
    for it in range(ITERS):
        drain(it)
    for d in range(2):
        pl.when(has_next(d))(lambda d=d: rec_copy(d).wait_send())
    for write in writes:
        write.wait()
    each(1, total, lambda s: chg_arrive(s).wait_recv())
    everyone = jnp.sum(chg[...], axis=0)
    share = 1.0 / (n_tm * n_arch * n_rep * nblk * block * seeds.shape[2])
    for it in range(ITERS):
        change[it] = jnp.sum(everyone[it : it + 1, :]) * share
    each(1, total, lambda s: chg_copy(s).wait_send())


def shards(seeds, band, band_mask, recording, cross, cross_ref, cross_mask):
    n_arch = lax.axis_size("archive")
    n_tm = lax.axis_size("tm")
    n_rep = lax.axis_size("replica")
    _, rows, width = seeds.shape
    nblk, block = band.shape[1], band.shape[3]
    slots = cross_ref.shape[2]
    nsub = nblk if n_tm * n_arch <= 16 else 1
    group = max(g for g in (4, 3, 2, 1) if slots % g == 0)
    total = n_tm * n_arch * n_rep
    held = (n_arch * n_tm * nblk + 1, block, width)
    need = 2 * held[0] * block * width * 2 + cross.size * 2 + band.size * 2 + 4 * seeds.size * 4
    need += total * 8 * width * 4
    dma = pltpu.SemaphoreType.DMA
    vmem = pl.BlockSpec(memory_space=pltpu.VMEM)
    smem = pl.BlockSpec(memory_space=pltpu.SMEM)
    hbm = pl.BlockSpec(memory_space=pl.ANY)
    labels, change = pl.pallas_call(
        functools.partial(kernel, (n_tm, n_arch, n_rep, nblk, block, slots, nsub, group)),
        out_shape=(
            jax.ShapeDtypeStruct(seeds.shape, jnp.float32),
            jax.ShapeDtypeStruct((ITERS,), jnp.float32),
        ),
        in_specs=[vmem, hbm, smem, vmem, hbm, smem, smem],
        out_specs=(hbm, smem),
        scratch_shapes=[
            pltpu.VMEM(held, jnp.bfloat16),
            pltpu.VMEM(held, jnp.bfloat16),
            pltpu.VMEM(cross.shape[1:], jnp.bfloat16),
            pltpu.VMEM(band.shape[1:], jnp.bfloat16),
            pltpu.VMEM((nblk, 8, block), jnp.int32),
            pltpu.VMEM((2, 8, block), jnp.int32),
            pltpu.VMEM((rows, width), jnp.float32),
            pltpu.VMEM((rows, width), jnp.float32),
            pltpu.VMEM((total, 8, width), jnp.float32),
            dma((1 + nblk,)),
            dma((ITERS, 2, n_tm + 1, nsub)),
            dma((ITERS, 2, n_tm + 1, nsub)),
            dma((ITERS, n_arch, n_tm, nsub)),
            dma((ITERS, n_arch, n_tm, nsub)),
            dma((2,)),
            dma((2,)),
            dma((total,)),
            dma((total,)),
            dma((nblk,)),
        ],
        compiler_params=pltpu.CompilerParams(
            collective_id=0,
            has_side_effects=True,
            vmem_limit_bytes=need + (8 << 20),
        ),
    )(seeds, band, band_mask, recording, cross, cross_ref, cross_mask)
    return labels, change


def solution(mesh):
    return jax.shard_map(
        shards,
        mesh=mesh,
        in_specs=(
            P(("groups", "archive"), "tm", "replica"),
            P(("groups", "archive"), "tm", None, None, None),
            P(("groups", "archive"), "tm", None),
            P(("groups", "archive"), "tm"),
            P(("groups", "archive"), "tm", None, None, None),
            P(("groups", "archive"), "tm", None),
            P(("groups", "archive"), "tm", None),
        ),
        out_specs=(P(("groups", "archive"), "tm", "replica"), P("groups")),
        check_vma=False,
    )
```

```python
import functools

import jax
import jax.numpy as jnp
from jax import lax
from jax.experimental import pallas as pl
from jax.experimental.pallas import tpu as pltpu
from jax.sharding import PartitionSpec as P

ITERS = 2
ALPHA = 0.85


def each(lo, hi, body):
    if hi - lo <= 16:
        for i in range(lo, hi):
            body(i)
    else:
        lax.fori_loop(lo, hi, lambda i, c: (body(i), c)[1], 0)


def kernel(
    dims,
    seeds_in,
    band,
    band_mask_in,
    recording_in,
    cross,
    cross_ref_in,
    cross_mask_in,
    out,
    change,
    seeds,
    recording,
    band_mask,
    cross_ref,
    cross_mask,
    lab0,
    lab1,
    cross_v,
    band_v,
    rec_s,
    rec_halo,
    current,
    scale,
    chg,
    in_sem,
    zs,
    zr,
    xs,
    xr,
    ds,
    dr_sem,
    rs,
    rr,
    cs,
    cr,
    out_sem,
):
    n_tm, n_arch, n_rep, nblk, block, slots, nsub, group, half = dims
    labs = (lab0, lab1)
    per = nblk // nsub
    t = lax.axis_index("tm")
    a = lax.axis_index("archive")
    r = lax.axis_index("replica")
    total = n_tm * n_arch * n_rep
    me = (t * n_arch + a) * n_rep + r
    zero_slot = n_arch * n_tm * nblk
    own = (a * n_tm + t) * nblk
    archive_lo = a * n_tm * nblk
    archive_hi = archive_lo + n_tm * nblk - 1
    MESH = pl.DeviceIdType.MESH

    def wrap(i, n):
        return jnp.where(i >= n, i - n, i)

    def offsets(step):
        return step // (n_arch * n_rep), (step // n_rep) % n_arch, step % n_rep

    def peer(step):
        dt, da, dr = offsets(step)
        return {"tm": wrap(t + dt, n_tm), "archive": wrap(a + da, n_arch), "replica": wrap(r + dr, n_rep)}

    small = [
        pltpu.make_async_copy(src, dst, in_sem.at[1 + nblk + i])
        for i, (src, dst) in enumerate(
            (
                (seeds_in, seeds),
                (recording_in, recording),
                (band_mask_in, band_mask),
                (cross_ref_in, cross_ref),
                (cross_mask_in, cross_mask),
            )
        )
    ]
    for load in small:
        load.start()
    loads = [pltpu.make_async_copy(band.at[0], band_v, in_sem.at[0])]
    for b in range(nblk):
        loads.append(pltpu.make_async_copy(cross.at[0, b], cross_v.at[b], in_sem.at[1 + b]))

    rec_halo[...] = jnp.full(rec_halo.shape, -1, jnp.int32)

    barrier = pltpu.get_barrier_semaphore()

    def greet(step):
        pl.semaphore_signal(barrier, inc=1, device_id=peer(step), device_id_type=MESH)

    each(1, total, greet)
    for load in loads:
        load.start()
    small[0].wait()
    small[1].wait()
    for b in range(nblk):
        rec_s[b] = jnp.broadcast_to(recording[:, b * block : (b + 1) * block], (8, block))
        lab0[own + b] = seeds[0, b * block : (b + 1) * block, :].astype(jnp.bfloat16)
    zeros = jnp.zeros((block, lab0.shape[2]), jnp.bfloat16)
    lab0[zero_slot] = zeros
    lab1[zero_slot] = zeros
    pl.semaphore_wait(barrier, total - 1)

    def z_copy(it, d, j, sub):
        src = t - j if d == 0 else t + j
        nxt = jnp.minimum(t + 1, n_tm - 1) if d == 0 else jnp.maximum(t - 1, 0)
        lab = labs[it]
        where = pl.ds((a * n_tm + src) * nblk + sub * per, per)
        return pltpu.make_async_remote_copy(
            src_ref=lab.at[where],
            dst_ref=lab.at[where],
            send_sem=zs.at[it, d, j, sub],
            recv_sem=zr.at[it, d, j + 1, sub],
            device_id={"tm": nxt},
            device_id_type=MESH,
        )

    def z_arrive(it, d, j, sub):
        src = t - j if d == 0 else t + j
        lab = labs[it]
        where = pl.ds((a * n_tm + src) * nblk + sub * per, per)
        return pltpu.make_async_remote_copy(
            src_ref=lab.at[where],
            dst_ref=lab.at[where],
            send_sem=zs.at[it, d, j, sub],
            recv_sem=zr.at[it, d, j, sub],
            device_id={"tm": wrap(t + 1, n_tm)},
            device_id_type=MESH,
        )

    def x_copy(it, m, src, sub):
        lab = labs[it]
        where = pl.ds((a * n_tm + src) * nblk + sub * per, per)
        return pltpu.make_async_remote_copy(
            src_ref=lab.at[where],
            dst_ref=lab.at[where],
            send_sem=xs.at[it, m, src, sub],
            recv_sem=xr.at[it, m, src, sub],
            device_id={"archive": wrap(a + m, n_arch)},
            device_id_type=MESH,
        )

    def x_arrive(it, m, src, sub):
        lab = labs[it]
        frm = wrap(a + n_arch - m, n_arch)
        where = pl.ds((frm * n_tm + src) * nblk + sub * per, per)
        return pltpu.make_async_remote_copy(
            src_ref=lab.at[where],
            dst_ref=lab.at[where],
            send_sem=xs.at[it, m, src, sub],
            recv_sem=xr.at[it, m, src, sub],
            device_id={"archive": wrap(a + m, n_arch)},
            device_id_type=MESH,
        )

    def has_next(d):
        return t + 1 < n_tm if d == 0 else t >= 1

    def has_source(d, j):
        return t >= j if d == 0 else t + j < n_tm

    last = n_tm - 1
    at_end = (t == 0) | (t == last)

    def direct(src, sub):
        if sub >= half:
            return None
        far = jnp.where((t == 0) | (t == 2), last, 0)
        return src != far

    def guarded(cond, body):
        if cond is None:
            body()
        else:
            pl.when(cond)(body)

    def detour(it, kind, sub, arriving):
        if arriving:
            src = jnp.where((t == 0) | (t == 2), last, 0)
        elif kind == 0:
            src = t
        else:
            src = jnp.where(t == 1, last, 0)
        lab = labs[it]
        where = pl.ds(((1 - a) * n_tm + src) * nblk + sub * per, per)
        return pltpu.make_async_remote_copy(
            src_ref=lab.at[where],
            dst_ref=lab.at[where],
            send_sem=ds.at[it, kind, sub],
            recv_sem=dr_sem.at[it, kind, sub],
            device_id={"tm": jnp.where(t < 2, 1 - t, 5 - t)},
            device_id_type=MESH,
        )

    def sends_kind(kind):
        return at_end if kind == 0 else jnp.logical_not(at_end)

    def detour_send(it, kind):
        for sub in range(half):

            @pl.when(sends_kind(kind))
            def _():
                src = t if kind == 0 else jnp.where(t == 1, last, 0)
                x_arrive(it, 1, src, sub).wait_recv()
                detour(it, kind, sub, False).start()

    def x_send(it, src, sub):
        guarded(
            direct(src, sub),
            lambda: each(1, n_arch, lambda m: x_copy(it, m, src, sub).start()),
        )

    def own_send(it, sub):
        for d in range(2):
            pl.when(has_next(d))(lambda d=d: z_copy(it, d, 0, sub).start())
        each(1, n_arch, lambda m: x_copy(it, m, t, sub).start())

    def hand_on(it, j, sub):
        for d in (1, 0):

            @pl.when(has_source(d, j))
            def _():
                src = t - j if d == 0 else t + j
                z_arrive(it, d, j, sub).wait_recv()
                pl.when(has_next(d))(lambda: z_copy(it, d, j, sub).start())
                x_send(it, src, sub)

    def x_wait(it):
        def one(src):
            for sub in range(nsub):
                if sub < half and src in (0, last):
                    continue
                each(1, n_arch, lambda m: x_arrive(it, m, src, sub).wait_recv())

        each(0, n_tm, one)
        for sub in range(half):
            for kind in range(2):
                pl.when(sends_kind(1 - kind))(
                    lambda kind=kind: detour(it, kind, sub, True).wait_recv()
                )

    def drain(it):
        def one(src):
            for sub in range(nsub):
                guarded(
                    direct(src, sub),
                    lambda: each(1, n_arch, lambda m: x_copy(it, m, src, sub).wait_send()),
                )

        each(0, n_tm, one)

        def hop(j):
            for d in range(2):
                go = has_next(d) & has_source(d, j)

                @pl.when(go)
                def _():
                    for sub in range(nsub):
                        z_copy(it, d, j, sub).wait_send()

        each(0, n_tm, hop)
        for sub in range(half):
            for kind in range(2):
                pl.when(sends_kind(kind))(
                    lambda kind=kind: detour(it, kind, sub, False).wait_send()
                )

    def rec_copy(d):
        return pltpu.make_async_remote_copy(
            src_ref=rec_s.at[nblk - 1 if d == 0 else 0],
            dst_ref=rec_halo.at[d],
            send_sem=rs.at[d],
            recv_sem=rr.at[d],
            device_id={"tm": jnp.minimum(t + 1, n_tm - 1) if d == 0 else jnp.maximum(t - 1, 0)},
            device_id_type=MESH,
        )

    for d in range(2):
        pl.when(has_next(d))(lambda d=d: rec_copy(d).start())
    for sub in range(nsub):
        own_send(0, sub)
    for load in small[2:]:
        load.wait()

    def rows(b):
        return pl.ds(b * block, block)


    def cross_degree(b):
        loads[1 + b].wait()
        acc = jnp.zeros((block, block), jnp.float32)
        for k in range(slots):
            live = (cross_mask[0, b, k] > 0).astype(jnp.float32)
            acc += cross_v[b, k].astype(jnp.float32) * live
        scale[rows(b), :] = acc

    def band_weights(b):
        acc = scale[rows(b), :]
        mine = jnp.broadcast_to(rec_s[b, 0:1, :], (block, block)).astype(jnp.float32).T
        for o in range(3):
            near = b + o - 1
            if near < 0:
                theirs = rec_halo[0, 0:1, :]
            elif near >= nblk:
                theirs = rec_halo[1, 0:1, :]
            else:
                theirs = rec_s[near, 0:1, :]
            theirs = jnp.where(band_mask[o, 0, b] > 0, theirs, -2).astype(jnp.float32)
            w = jnp.where(mine == theirs, band_v[b, o].astype(jnp.float32), 0.0)
            band_v[b, o] = w.astype(jnp.bfloat16)
            acc += w
        degree = jnp.sum(acc, axis=1, keepdims=True)
        scale[rows(b), :] = jnp.broadcast_to(ALPHA / (1.0 + degree), (block, scale.shape[1]))

    def spread_of(it, b):
        lab = labs[it]
        near = [jnp.clip(own + b + o - 1, archive_lo, archive_hi) for o in range(3)]
        acc = jnp.dot(
            jnp.concatenate([band_v[b, o] for o in range(3)], axis=1),
            jnp.concatenate([lab[i] for i in near], axis=0),
            preferred_element_type=jnp.float32,
        )
        for k0 in range(0, slots, group):
            ks = range(k0, k0 + group)
            spots = [jnp.where(cross_mask[0, b, k] > 0, cross_ref[0, b, k], zero_slot) for k in ks]
            acc += jnp.dot(
                jnp.concatenate([cross_v[b, k] for k in ks], axis=1),
                jnp.concatenate([lab[i] for i in spots], axis=0),
                preferred_element_type=jnp.float32,
            )
        return acc

    def step(it, b):
        spread = spread_of(it, b)
        first = seeds[0, rows(b), :]
        before = first if it == 0 else current[rows(b), :]
        updated = (1.0 - ALPHA) * first + (before + spread) * scale[rows(b), :]
        current[rows(b), :] = updated
        if it + 1 < ITERS:
            labs[it + 1][own + b] = updated.astype(jnp.bfloat16)
        diff = updated - before
        return jnp.sum(diff * diff, axis=0, keepdims=True)

    def neighbours():
        loads[0].wait()
        for d in range(2):
            pl.when(has_source(d, 1))(lambda d=d: rec_copy(d).wait_recv())

    work = [functools.partial(cross_degree, b) for b in range(nblk)]
    work.append(neighbours)
    work += [functools.partial(band_weights, b) for b in range(nblk)]

    def later(it, lo):
        def one(j):
            for sub in range(nsub):
                hand_on(it, j, sub)

        each(lo, n_tm, one)

    def do(count):
        for _ in range(min(count, len(work))):
            work.pop(0)()

    do(2)
    for sub in range(nsub):
        hand_on(0, 1, sub)
        do(1)
    detour_send(0, 0)
    if n_tm == 4:
        for sub in range(nsub):
            hand_on(0, 2, sub)
            do(2)
        detour_send(0, 1)
        do(len(work))
        later(0, 3)
    else:
        do(len(work))
        later(0, 2)
    x_wait(0)

    sums = jnp.zeros((1, seeds.shape[2]), jnp.float32)
    for sub in range(nsub):
        for b in range(sub * per, (sub + 1) * per):
            sums += step(0, b)
        own_send(1, sub)
        if sub >= 1:
            hand_on(1, 1, sub - 1)
    hand_on(1, 1, nsub - 1)
    detour_send(1, 0)
    if n_tm == 4:
        for sub in range(nsub):
            hand_on(1, 2, sub)
        detour_send(1, 1)
        later(1, 3)
    else:
        later(1, 2)
    x_wait(1)
    totals = [sums]
    sums = jnp.zeros((1, seeds.shape[2]), jnp.float32)
    writes = []
    for b in range(nblk):
        sums += step(1, b)
        writes.append(
            pltpu.make_async_copy(current.at[rows(b)], out.at[0, rows(b)], out_sem.at[b])
        )
        writes[-1].start()
    totals.append(sums)

    row = lax.broadcasted_iota(jnp.int32, (8, seeds.shape[2]), 0)
    chg[me] = jnp.where(row == 0, totals[0], jnp.where(row == 1, totals[1], 0.0))

    def chg_copy(s):
        return pltpu.make_async_remote_copy(
            src_ref=chg.at[me],
            dst_ref=chg.at[me],
            send_sem=cs.at[s],
            recv_sem=cr.at[s],
            device_id=peer(s),
            device_id_type=MESH,
        )

    def chg_arrive(s):
        dt, da, dr = offsets(s)
        frm = wrap(t + n_tm - dt, n_tm) * n_arch + wrap(a + n_arch - da, n_arch)
        frm = frm * n_rep + wrap(r + n_rep - dr, n_rep)
        return pltpu.make_async_remote_copy(
            src_ref=chg.at[frm],
            dst_ref=chg.at[frm],
            send_sem=cs.at[s],
            recv_sem=cr.at[s],
            device_id=peer(s),
            device_id_type=MESH,
        )

    each(1, total, lambda s: chg_copy(s).start())
    for it in range(ITERS):
        drain(it)
    for d in range(2):
        pl.when(has_next(d))(lambda d=d: rec_copy(d).wait_send())
    for write in writes:
        write.wait()
    each(1, total, lambda s: chg_arrive(s).wait_recv())
    everyone = jnp.sum(chg[...], axis=0)
    share = 1.0 / (n_tm * n_arch * n_rep * nblk * block * seeds.shape[2])
    for it in range(ITERS):
        change[it] = jnp.sum(everyone[it : it + 1, :]) * share
    each(1, total, lambda s: chg_copy(s).wait_send())


def shards(seeds, band, band_mask, recording, cross, cross_ref, cross_mask):
    n_arch = lax.axis_size("archive")
    n_tm = lax.axis_size("tm")
    n_rep = lax.axis_size("replica")
    _, rows, width = seeds.shape
    nblk, block = band.shape[1], band.shape[3]
    slots = cross_ref.shape[2]
    nsub = 2 if n_tm * n_arch <= 16 and nblk % 2 == 0 else 1
    half = 0
    group = max(g for g in (4, 3, 2, 1) if slots % g == 0)
    total = n_tm * n_arch * n_rep
    band_mask = jnp.transpose(band_mask, (2, 0, 1))
    held = (n_arch * n_tm * nblk + 1, block, width)
    dma = pltpu.SemaphoreType.DMA
    smem = pl.BlockSpec(memory_space=pltpu.SMEM)
    hbm = pl.BlockSpec(memory_space=pl.ANY)
    labels, change = pl.pallas_call(
        functools.partial(kernel, (n_tm, n_arch, n_rep, nblk, block, slots, nsub, group, half)),
        out_shape=(
            jax.ShapeDtypeStruct(seeds.shape, jnp.float32),
            jax.ShapeDtypeStruct((ITERS,), jnp.float32),
        ),
        in_specs=[hbm] * 7,
        out_specs=(hbm, smem),
        scratch_shapes=[
            pltpu.VMEM(seeds.shape, jnp.float32),
            pltpu.VMEM(recording.shape, jnp.int32),
            pltpu.SMEM(band_mask.shape, jnp.int32),
            pltpu.SMEM(cross_ref.shape, jnp.int32),
            pltpu.SMEM(cross_mask.shape, jnp.int32),
            pltpu.VMEM(held, jnp.bfloat16),
            pltpu.VMEM(held, jnp.bfloat16),
            pltpu.VMEM(cross.shape[1:], jnp.bfloat16),
            pltpu.VMEM(band.shape[1:], jnp.bfloat16),
            pltpu.VMEM((nblk, 8, block), jnp.int32),
            pltpu.VMEM((2, 8, block), jnp.int32),
            pltpu.VMEM((rows, width), jnp.float32),
            pltpu.VMEM((rows, width), jnp.float32),
            pltpu.VMEM((total, 8, width), jnp.float32),
            dma((6 + nblk,)),
            dma((ITERS, 2, n_tm + 1, nsub)),
            dma((ITERS, 2, n_tm + 1, nsub)),
            dma((ITERS, n_arch, n_tm, nsub)),
            dma((ITERS, n_arch, n_tm, nsub)),
            dma((ITERS, 2, nsub)),
            dma((ITERS, 2, nsub)),
            dma((2,)),
            dma((2,)),
            dma((total,)),
            dma((total,)),
            dma((nblk,)),
        ],
        compiler_params=pltpu.CompilerParams(
            collective_id=0,
            has_side_effects=True,
            vmem_limit_bytes=63 << 20,
        ),
    )(seeds, band, band_mask, recording, cross, cross_ref, cross_mask)
    return labels, change


def solution(mesh):
    return jax.shard_map(
        shards,
        mesh=mesh,
        in_specs=(
            P(("groups", "archive"), "tm", "replica"),
            P(("groups", "archive"), "tm", None, None, None),
            P(("groups", "archive"), "tm", None),
            P(("groups", "archive"), "tm"),
            P(("groups", "archive"), "tm", None, None, None),
            P(("groups", "archive"), "tm", None),
            P(("groups", "archive"), "tm", None),
        ),
        out_specs=(P(("groups", "archive"), "tm", "replica"), P("groups")),
        check_vma=False,
    )
```

```python
import functools

import jax
import jax.numpy as jnp
from jax import lax
from jax.experimental import pallas as pl
from jax.experimental.pallas import tpu as pltpu
from jax.sharding import PartitionSpec as P

ITERS = 2
ALPHA = 0.85


def each(lo, hi, body):
    if hi - lo <= 16:
        for i in range(lo, hi):
            body(i)
    else:
        lax.fori_loop(lo, hi, lambda i, c: (body(i), c)[1], 0)


def kernel(
    dims,
    seeds_in,
    band,
    band_mask_in,
    recording_in,
    cross,
    cross_ref_in,
    cross_mask_in,
    out,
    change,
    seeds,
    recording,
    band_mask,
    cross_ref,
    cross_mask,
    lab0,
    lab1,
    cross_v,
    band_v,
    rec_s,
    rec_halo,
    current,
    scale,
    chg,
    in_sem,
    zs,
    zr,
    xs,
    xr,
    ds,
    dr_sem,
    rs,
    rr,
    cs,
    cr,
    out_sem,
):
    n_tm, n_arch, n_rep, nblk, block, slots, nsub, group, half = dims
    labs = (lab0, lab1)
    per = nblk // nsub
    t = lax.axis_index("tm")
    a = lax.axis_index("archive")
    r = lax.axis_index("replica")
    total = n_tm * n_arch * n_rep
    me = (t * n_arch + a) * n_rep + r
    zero_slot = n_arch * n_tm * nblk
    own = (a * n_tm + t) * nblk
    archive_lo = a * n_tm * nblk
    archive_hi = archive_lo + n_tm * nblk - 1
    MESH = pl.DeviceIdType.MESH

    def wrap(i, n):
        return jnp.where(i >= n, i - n, i)

    def offsets(step):
        return step // (n_arch * n_rep), (step // n_rep) % n_arch, step % n_rep

    def peer(step):
        dt, da, dr = offsets(step)
        return {"tm": wrap(t + dt, n_tm), "archive": wrap(a + da, n_arch), "replica": wrap(r + dr, n_rep)}

    small = [
        pltpu.make_async_copy(src, dst, in_sem.at[1 + nblk + i])
        for i, (src, dst) in enumerate(
            (
                (seeds_in, seeds),
                (recording_in, recording),
                (band_mask_in, band_mask),
                (cross_ref_in, cross_ref),
                (cross_mask_in, cross_mask),
            )
        )
    ]
    for load in small:
        load.start()
    loads = [pltpu.make_async_copy(band.at[0], band_v, in_sem.at[0])]
    for b in range(nblk):
        loads.append(pltpu.make_async_copy(cross.at[0, b], cross_v.at[b], in_sem.at[1 + b]))

    rec_halo[...] = jnp.full(rec_halo.shape, -1, jnp.int32)

    barrier = pltpu.get_barrier_semaphore()

    def greet(step):
        pl.semaphore_signal(barrier, inc=1, device_id=peer(step), device_id_type=MESH)

    each(1, total, greet)
    for load in loads:
        load.start()
    small[0].wait()
    small[1].wait()
    for b in range(nblk):
        rec_s[b] = jnp.broadcast_to(recording[:, b * block : (b + 1) * block], (8, block))
        lab0[own + b] = seeds[0, b * block : (b + 1) * block, :].astype(jnp.bfloat16)
    zeros = jnp.zeros((block, lab0.shape[2]), jnp.bfloat16)
    lab0[zero_slot] = zeros
    lab1[zero_slot] = zeros
    pl.semaphore_wait(barrier, total - 1)

    def z_copy(it, d, j, sub):
        src = t - j if d == 0 else t + j
        nxt = jnp.minimum(t + 1, n_tm - 1) if d == 0 else jnp.maximum(t - 1, 0)
        lab = labs[it]
        where = pl.ds((a * n_tm + src) * nblk + sub * per, per)
        return pltpu.make_async_remote_copy(
            src_ref=lab.at[where],
            dst_ref=lab.at[where],
            send_sem=zs.at[it, d, j, sub],
            recv_sem=zr.at[it, d, j + 1, sub],
            device_id={"tm": nxt},
            device_id_type=MESH,
        )

    def z_arrive(it, d, j, sub):
        src = t - j if d == 0 else t + j
        lab = labs[it]
        where = pl.ds((a * n_tm + src) * nblk + sub * per, per)
        return pltpu.make_async_remote_copy(
            src_ref=lab.at[where],
            dst_ref=lab.at[where],
            send_sem=zs.at[it, d, j, sub],
            recv_sem=zr.at[it, d, j, sub],
            device_id={"tm": wrap(t + 1, n_tm)},
            device_id_type=MESH,
        )

    def x_copy(it, m, src, sub):
        lab = labs[it]
        where = pl.ds((a * n_tm + src) * nblk + sub * per, per)
        return pltpu.make_async_remote_copy(
            src_ref=lab.at[where],
            dst_ref=lab.at[where],
            send_sem=xs.at[it, m, src, sub],
            recv_sem=xr.at[it, m, src, sub],
            device_id={"archive": wrap(a + m, n_arch)},
            device_id_type=MESH,
        )

    def x_arrive(it, m, src, sub):
        lab = labs[it]
        frm = wrap(a + n_arch - m, n_arch)
        where = pl.ds((frm * n_tm + src) * nblk + sub * per, per)
        return pltpu.make_async_remote_copy(
            src_ref=lab.at[where],
            dst_ref=lab.at[where],
            send_sem=xs.at[it, m, src, sub],
            recv_sem=xr.at[it, m, src, sub],
            device_id={"archive": wrap(a + m, n_arch)},
            device_id_type=MESH,
        )

    def has_next(d):
        return t + 1 < n_tm if d == 0 else t >= 1

    def has_source(d, j):
        return t >= j if d == 0 else t + j < n_tm

    last = n_tm - 1
    at_end = (t == 0) | (t == last)

    def direct(src, sub):
        if sub >= half:
            return None
        far = jnp.where((t == 0) | (t == 2), last, 0)
        return src != far

    def guarded(cond, body):
        if cond is None:
            body()
        else:
            pl.when(cond)(body)

    def detour(it, kind, sub, arriving):
        if arriving:
            src = jnp.where((t == 0) | (t == 2), last, 0)
        elif kind == 0:
            src = t
        else:
            src = jnp.where(t == 1, last, 0)
        lab = labs[it]
        where = pl.ds(((1 - a) * n_tm + src) * nblk + sub * per, per)
        return pltpu.make_async_remote_copy(
            src_ref=lab.at[where],
            dst_ref=lab.at[where],
            send_sem=ds.at[it, kind, sub],
            recv_sem=dr_sem.at[it, kind, sub],
            device_id={"tm": jnp.where(t < 2, 1 - t, 5 - t)},
            device_id_type=MESH,
        )

    def sends_kind(kind):
        return at_end if kind == 0 else jnp.logical_not(at_end)

    def detour_send(it, kind):
        for sub in range(half):

            @pl.when(sends_kind(kind))
            def _():
                src = t if kind == 0 else jnp.where(t == 1, last, 0)
                x_arrive(it, 1, src, sub).wait_recv()
                detour(it, kind, sub, False).start()

    def x_send(it, src, sub):
        guarded(
            direct(src, sub),
            lambda: each(1, n_arch, lambda m: x_copy(it, m, src, sub).start()),
        )

    def own_send(it, sub):
        for d in range(2):
            pl.when(has_next(d))(lambda d=d: z_copy(it, d, 0, sub).start())
        each(1, n_arch, lambda m: x_copy(it, m, t, sub).start())

    def hand_on(it, j, sub):
        for d in (1, 0):

            @pl.when(has_source(d, j))
            def _():
                src = t - j if d == 0 else t + j
                z_arrive(it, d, j, sub).wait_recv()
                pl.when(has_next(d))(lambda: z_copy(it, d, j, sub).start())
                x_send(it, src, sub)

    def x_wait(it):
        def one(src):
            for sub in range(nsub):
                if sub < half and src in (0, last):
                    continue
                each(1, n_arch, lambda m: x_arrive(it, m, src, sub).wait_recv())

        each(0, n_tm, one)
        for sub in range(half):
            for kind in range(2):
                pl.when(sends_kind(1 - kind))(
                    lambda kind=kind: detour(it, kind, sub, True).wait_recv()
                )

    def drain(it):
        def one(src):
            for sub in range(nsub):
                guarded(
                    direct(src, sub),
                    lambda: each(1, n_arch, lambda m: x_copy(it, m, src, sub).wait_send()),
                )

        each(0, n_tm, one)

        def hop(j):
            for d in range(2):
                go = has_next(d) & has_source(d, j)

                @pl.when(go)
                def _():
                    for sub in range(nsub):
                        z_copy(it, d, j, sub).wait_send()

        each(0, n_tm, hop)
        for sub in range(half):
            for kind in range(2):
                pl.when(sends_kind(kind))(
                    lambda kind=kind: detour(it, kind, sub, False).wait_send()
                )

    def rec_copy(d):
        return pltpu.make_async_remote_copy(
            src_ref=rec_s.at[nblk - 1 if d == 0 else 0],
            dst_ref=rec_halo.at[d],
            send_sem=rs.at[d],
            recv_sem=rr.at[d],
            device_id={"tm": jnp.minimum(t + 1, n_tm - 1) if d == 0 else jnp.maximum(t - 1, 0)},
            device_id_type=MESH,
        )

    for d in range(2):
        pl.when(has_next(d))(lambda d=d: rec_copy(d).start())
    for sub in range(nsub):
        own_send(0, sub)
    for load in small[2:]:
        load.wait()

    def rows(b):
        return pl.ds(b * block, block)


    def cross_degree(b):
        loads[1 + b].wait()
        acc = jnp.zeros((block, block), jnp.float32)
        for k in range(slots):
            live = (cross_mask[0, b, k] > 0).astype(jnp.float32)
            acc += cross_v[b, k].astype(jnp.float32) * live
        scale[rows(b), :] = acc

    def band_weights(b):
        acc = scale[rows(b), :]
        mine = jnp.broadcast_to(rec_s[b, 0:1, :], (block, block)).astype(jnp.float32).T
        for o in range(3):
            near = b + o - 1
            if near < 0:
                theirs = rec_halo[0, 0:1, :]
            elif near >= nblk:
                theirs = rec_halo[1, 0:1, :]
            else:
                theirs = rec_s[near, 0:1, :]
            theirs = jnp.where(band_mask[o, 0, b] > 0, theirs, -2).astype(jnp.float32)
            w = jnp.where(mine == theirs, band_v[b, o].astype(jnp.float32), 0.0)
            band_v[b, o] = w.astype(jnp.bfloat16)
            acc += w
        degree = jnp.sum(acc, axis=1, keepdims=True)
        scale[rows(b), :] = jnp.broadcast_to(ALPHA / (1.0 + degree), (block, scale.shape[1]))

    def spread_of(it, b):
        lab = labs[it]
        near = [jnp.clip(own + b + o - 1, archive_lo, archive_hi) for o in range(3)]
        acc = jnp.dot(
            jnp.concatenate([band_v[b, o] for o in range(3)], axis=1),
            jnp.concatenate([lab[i] for i in near], axis=0),
            preferred_element_type=jnp.float32,
        )
        for k0 in range(0, slots, group):
            ks = range(k0, k0 + group)
            spots = [jnp.where(cross_mask[0, b, k] > 0, cross_ref[0, b, k], zero_slot) for k in ks]
            acc += jnp.dot(
                jnp.concatenate([cross_v[b, k] for k in ks], axis=1),
                jnp.concatenate([lab[i] for i in spots], axis=0),
                preferred_element_type=jnp.float32,
            )
        return acc

    def step(it, b):
        spread = spread_of(it, b)
        first = seeds[0, rows(b), :]
        before = first if it == 0 else current[rows(b), :]
        updated = (1.0 - ALPHA) * first + (before + spread) * scale[rows(b), :]
        current[rows(b), :] = updated
        if it + 1 < ITERS:
            labs[it + 1][own + b] = updated.astype(jnp.bfloat16)
        diff = updated - before
        return jnp.sum(diff * diff, axis=0, keepdims=True)

    def neighbours():
        loads[0].wait()
        for d in range(2):
            pl.when(has_source(d, 1))(lambda d=d: rec_copy(d).wait_recv())

    work = [functools.partial(cross_degree, b) for b in range(nblk)]
    work.append(neighbours)
    work += [functools.partial(band_weights, b) for b in range(nblk)]

    def later(it, lo):
        def one(j):
            for sub in range(nsub):
                hand_on(it, j, sub)

        each(lo, n_tm, one)

    def do(count):
        for _ in range(min(count, len(work))):
            work.pop(0)()

    do(2)
    for sub in range(nsub):
        hand_on(0, 1, sub)
        do(1)
    detour_send(0, 0)
    if n_tm == 4:
        for sub in range(nsub):
            hand_on(0, 2, sub)
            do(2)
        detour_send(0, 1)
        do(len(work))
        later(0, 3)
    else:
        do(len(work))
        later(0, 2)
    x_wait(0)

    sums = jnp.zeros((1, seeds.shape[2]), jnp.float32)
    for sub in range(nsub):
        for b in range(sub * per, (sub + 1) * per):
            sums += step(0, b)
        own_send(1, sub)
        if sub >= 1:
            hand_on(1, 1, sub - 1)
    hand_on(1, 1, nsub - 1)
    detour_send(1, 0)
    if n_tm == 4:
        for sub in range(nsub):
            hand_on(1, 2, sub)
        detour_send(1, 1)
        later(1, 3)
    else:
        later(1, 2)
    drain(0)
    x_wait(1)
    totals = [sums]
    sums = jnp.zeros((1, seeds.shape[2]), jnp.float32)
    writes = []
    for b in range(nblk):
        sums += step(1, b)
        writes.append(
            pltpu.make_async_copy(current.at[rows(b)], out.at[0, rows(b)], out_sem.at[b])
        )
        writes[-1].start()
    totals.append(sums)

    row = lax.broadcasted_iota(jnp.int32, (8, seeds.shape[2]), 0)
    chg[me] = jnp.where(row == 0, totals[0], jnp.where(row == 1, totals[1], 0.0))

    def chg_copy(s):
        return pltpu.make_async_remote_copy(
            src_ref=chg.at[me],
            dst_ref=chg.at[me],
            send_sem=cs.at[s],
            recv_sem=cr.at[s],
            device_id=peer(s),
            device_id_type=MESH,
        )

    def chg_arrive(s):
        dt, da, dr = offsets(s)
        frm = wrap(t + n_tm - dt, n_tm) * n_arch + wrap(a + n_arch - da, n_arch)
        frm = frm * n_rep + wrap(r + n_rep - dr, n_rep)
        return pltpu.make_async_remote_copy(
            src_ref=chg.at[frm],
            dst_ref=chg.at[frm],
            send_sem=cs.at[s],
            recv_sem=cr.at[s],
            device_id=peer(s),
            device_id_type=MESH,
        )

    each(1, total, lambda s: chg_copy(s).start())
    drain(1)
    for d in range(2):
        pl.when(has_next(d))(lambda d=d: rec_copy(d).wait_send())
    for write in writes:
        write.wait()
    each(1, total, lambda s: chg_arrive(s).wait_recv())
    everyone = jnp.sum(chg[...], axis=0)
    share = 1.0 / (n_tm * n_arch * n_rep * nblk * block * seeds.shape[2])
    for it in range(ITERS):
        change[it] = jnp.sum(everyone[it : it + 1, :]) * share
    each(1, total, lambda s: chg_copy(s).wait_send())


def shards(seeds, band, band_mask, recording, cross, cross_ref, cross_mask):
    n_arch = lax.axis_size("archive")
    n_tm = lax.axis_size("tm")
    n_rep = lax.axis_size("replica")
    _, rows, width = seeds.shape
    nblk, block = band.shape[1], band.shape[3]
    slots = cross_ref.shape[2]
    nsub = 2 if n_tm * n_arch <= 16 and nblk % 2 == 0 else 1
    half = 0
    group = max(g for g in (4, 3, 2, 1) if slots % g == 0)
    total = n_tm * n_arch * n_rep
    band_mask = jnp.transpose(band_mask, (2, 0, 1))
    held = (n_arch * n_tm * nblk + 1, block, width)
    dma = pltpu.SemaphoreType.DMA
    smem = pl.BlockSpec(memory_space=pltpu.SMEM)
    hbm = pl.BlockSpec(memory_space=pl.ANY)
    labels, change = pl.pallas_call(
        functools.partial(kernel, (n_tm, n_arch, n_rep, nblk, block, slots, nsub, group, half)),
        out_shape=(
            jax.ShapeDtypeStruct(seeds.shape, jnp.float32),
            jax.ShapeDtypeStruct((ITERS,), jnp.float32),
        ),
        in_specs=[hbm] * 7,
        out_specs=(hbm, smem),
        scratch_shapes=[
            pltpu.VMEM(seeds.shape, jnp.float32),
            pltpu.VMEM(recording.shape, jnp.int32),
            pltpu.SMEM(band_mask.shape, jnp.int32),
            pltpu.SMEM(cross_ref.shape, jnp.int32),
            pltpu.SMEM(cross_mask.shape, jnp.int32),
            pltpu.VMEM(held, jnp.bfloat16),
            pltpu.VMEM(held, jnp.bfloat16),
            pltpu.VMEM(cross.shape[1:], jnp.bfloat16),
            pltpu.VMEM(band.shape[1:], jnp.bfloat16),
            pltpu.VMEM((nblk, 8, block), jnp.int32),
            pltpu.VMEM((2, 8, block), jnp.int32),
            pltpu.VMEM((rows, width), jnp.float32),
            pltpu.VMEM((rows, width), jnp.float32),
            pltpu.VMEM((total, 8, width), jnp.float32),
            dma((6 + nblk,)),
            dma((ITERS, 2, n_tm + 1, nsub)),
            dma((ITERS, 2, n_tm + 1, nsub)),
            dma((ITERS, n_arch, n_tm, nsub)),
            dma((ITERS, n_arch, n_tm, nsub)),
            dma((ITERS, 2, nsub)),
            dma((ITERS, 2, nsub)),
            dma((2,)),
            dma((2,)),
            dma((total,)),
            dma((total,)),
            dma((nblk,)),
        ],
        compiler_params=pltpu.CompilerParams(
            collective_id=0,
            has_side_effects=True,
            vmem_limit_bytes=63 << 20,
        ),
    )(seeds, band, band_mask, recording, cross, cross_ref, cross_mask)
    return labels, change


def solution(mesh):
    return jax.shard_map(
        shards,
        mesh=mesh,
        in_specs=(
            P(("groups", "archive"), "tm", "replica"),
            P(("groups", "archive"), "tm", None, None, None),
            P(("groups", "archive"), "tm", None),
            P(("groups", "archive"), "tm"),
            P(("groups", "archive"), "tm", None, None, None),
            P(("groups", "archive"), "tm", None),
            P(("groups", "archive"), "tm", None),
        ),
        out_specs=(P(("groups", "archive"), "tm", "replica"), P("groups")),
        check_vma=False,
    )
```
